512 devices in a mesh: req: 16 (over y, core), ctx: 32 (over z, x).
Axes of the slice: x: 4, y: 8, z: 8, core: 2. Of those that a mesh axis runs over, the one named last changes fastest.
Arguments:
- latent_cache: bfloat16 [917504, 512], P(('req', 'ctx')), parts along dimension 0, may hold values from -6 to 6
- rope_cache: bfloat16 [917504, 64], P(('req', 'ctx')), parts along dimension 0, may hold values from -6 to 6
- lengths: int32 [32], P('req'), parts along dimension 0, may hold values from 1 to 35840, 57344 in all
- target_shard: int32 [917504], P(('req', 'ctx')), parts along dimension 0, may hold values from 0 to 31, as said below
- query_nope: bfloat16 [2, 32, 64, 128], P(None, 'req', 'ctx'), parts along dimension 1, may hold values from -12 to 12
- query_rope: bfloat16 [2, 32, 64, 64], P(None, 'req', 'ctx'), parts along dimension 1, may hold values from -400 to 400
- new_latent: bfloat16 [2, 32, 512], P(None, 'req'), parts along dimension 1, may hold values from -6 to 6
- new_rope: bfloat16 [2, 32, 64], P(None, 'req'), parts along dimension 1, may hold values from -6 to 6
- key_absorb: bfloat16 [64, 128, 512], P('ctx'), may hold values from -0.5 to 0.5
- value_up: bfloat16 [64, 512, 128], P('ctx'), may hold values from -0.25 to 0.25
Outputs:
- attention: bfloat16 [2, 32, 64, 128], P(None, 'req', 'ctx'), parts along dimension 1
- latent_decode: bfloat16 [917504, 512], P(('req', 'ctx')), parts along dimension 0
- rope_decode: bfloat16 [917504, 64], P(('req', 'ctx')), parts along dimension 0
The draws below stay inside these ranges and needn't reach their ends.
There are 16 independent parts, one for each index of `req`. The reference program is written for one: setup_inputs(seed, part) draws one part's arguments, and reference() takes and returns one part's arrays. A program takes and returns all parts, laid end to end along the dimension named above; an argument that names none is the same for every part. Nothing has to cross between parts.
Inputs may be any that keep to these rules, and one draw needn't show every extreme that they name: `target_shard`: each aligned block of 1792 positions names every shard exactly 56 times.
All inputs are finite; a program needn't handle non-finite values.
Results may differ from the reference program's by a relative error of at most 0.019.
Values may be sent and summed in bfloat16 or wider, within the bound.
A program may use at most 128 MiB of HBM per device.

```python
import math
import jax
import jax.numpy as jnp
import numpy as np
from jax import lax

D_LAT = 512
D_ROPE = 64
D_NOPE = 128
D_V = 128
HEADS = 64
TOK_DEV = 1792
REQS = 2
STEPS = 2
TOKENS = 57344
N_CTX = 32


def base_rope(key):
    return jnp.clip(jax.random.normal(jax.random.fold_in(key, 11), (TOKENS, D_ROPE), jnp.float32), -6.0, 6.0)


def base_fresh(key):
    return jnp.clip(jax.random.normal(jax.random.fold_in(key, 12), (STEPS, REQS, D_ROPE), jnp.float32), -6.0, 6.0)


def draw_rope_cache(key, part):
    rope_rows = base_rope(key)
    return rope_rows.astype(jnp.bfloat16)


def draw_new_rope(key, part):
    return base_fresh(key).astype(jnp.bfloat16)


def draw_query_rope(key, part):
    fresh_rope = base_fresh(key)
    key = jax.random.fold_in(key, 5)
    jitter = jnp.clip(jax.random.normal(key, (STEPS, REQS, HEADS, D_ROPE), jnp.float32), -6.0, 6.0)
    queries = 3.5 * fresh_rope[:, :, None, :] + jitter
    return queries.astype(jnp.bfloat16)


def draw_target_shard(key, part):
    key = jax.random.fold_in(key, 7)
    pattern = jnp.tile(jnp.arange(N_CTX, dtype=jnp.int32), TOK_DEV // N_CTX)
    block_keys = jax.random.split(key, N_CTX)

    def shuffle(block_key):
        return jax.random.permutation(block_key, pattern)
    return jax.vmap(shuffle)(block_keys).reshape(TOKENS)


def level_of(stream_key, extent, cuts, low, largest):
    def one(axis_at, blocks):
        heights = jax.random.uniform(jax.random.fold_in(jax.random.fold_in(stream_key, 6), axis_at), (blocks,), jnp.float32, low / len(cuts), largest / len(cuts))
        return jnp.repeat(jnp.exp(heights), extent[axis_at] // blocks).reshape((-1,) + (1,) * (len(extent) - axis_at - 1))

    level = one(*cuts[0])
    for cut in cuts[1:]:
        level = level * one(*cut)
    return level


def split_up(amount, total, bound, slope):
    loads = [(1 << 20) // math.isqrt(standing ** slope) + 1 for standing in range(2, amount + 1)]
    surplus, holding = total - bound - (amount - 1), [1] * (amount - 1)
    while surplus > 0:
        free = [i for i in range(amount - 1) if holding[i] < bound]
        whole, budget = sum([loads[i] for i in free]), surplus
        for i in free:
            addition = min(bound - holding[i], max(1, budget * loads[i] // whole), surplus)
            holding[i] = holding[i] + addition
            surplus = surplus - addition
    return np.array([bound] + holding)


def ragged(key, count, total, bound, lean):
    if count == 2:
        one = jax.random.randint(key, (), max(1, total - bound), min(bound, total - 1) + 1)
        return jnp.stack([one, total - one])
    tallies = jnp.asarray(split_up(count, total, bound, lean), jnp.int32)
    twos = (count - 1) // 2
    source_of, receiver = tallies[1:1 + 2 * twos:2], tallies[2:2 + 2 * twos:2]
    slack = jnp.minimum(source_of - 1, bound - receiver)
    moved = jax.random.randint(jax.random.fold_in(key, 1), (twos,), 0, 1 << 20) % (slack + 1)
    tallies = tallies.at[1:1 + 2 * twos:2].set(source_of - moved).at[2:2 + 2 * twos:2].set(receiver + moved)
    return tallies[jax.random.permutation(jax.random.fold_in(key, 2), count)]


def scatter_about(stream_key, extent, scale, bound, cuts=(), held_as=jnp.bfloat16):
    values = jax.random.normal(stream_key, extent, jnp.float32) * scale
    if len(cuts) > 0:
        values = level_of(stream_key, extent, cuts, -0.22, 0.18) * values
    return jnp.clip(values, min=-bound, max=bound).astype(held_as)


def setup_inputs(seed: int = 0, part: int = 0) -> dict:
    key_of = jax.random.split(jax.random.key(seed), 11)
    part_keys = jax.random.split(jax.random.fold_in(key_of[10], part), 11)
    latent_cache = scatter_about(part_keys[0], (TOKENS, D_LAT), 1.0, 6.0, ((0, 32),))
    rope_cache = draw_rope_cache(jax.random.fold_in(jax.random.fold_in(key_of[10], part), 71), part)
    lengths = ragged(part_keys[2], REQS, TOKENS, TOKENS * 5 // 8, 0).astype(jnp.int32)
    target_shard = draw_target_shard(jax.random.fold_in(jax.random.fold_in(key_of[10], part), 71), part)
    query_nope = scatter_about(part_keys[4], (STEPS, REQS, HEADS, D_NOPE), 2.0, 12.0, ((2, 32),))
    query_rope = draw_query_rope(jax.random.fold_in(jax.random.fold_in(key_of[10], part), 71), part)
    new_latent = scatter_about(part_keys[6], (STEPS, REQS, D_LAT), 1.0, 6.0)
    new_rope = draw_new_rope(jax.random.fold_in(jax.random.fold_in(key_of[10], part), 71), part)
    key_absorb = scatter_about(key_of[8], (HEADS, D_NOPE, D_LAT), D_NOPE ** -0.5, 0.5, ((0, 32),))
    value_up = scatter_about(key_of[9], (HEADS, D_LAT, D_V), D_LAT ** -0.5, 0.25, ((0, 32),))
    return {"latent_cache": latent_cache, "rope_cache": rope_cache, "lengths": lengths, "target_shard": target_shard, "query_nope": query_nope, "query_rope": query_rope, "new_latent": new_latent, "new_rope": new_rope, "key_absorb": key_absorb, "value_up": value_up}


NEG = -1e+30

def request_of(positions, lengths):
    bounds = jnp.cumsum(lengths)[:-1]
    return lax.optimization_barrier(jnp.sum((positions[:, None] >= bounds[None, :]).astype(jnp.int32), axis=1))

def reference(latent_cache, rope_cache, lengths, target_shard, query_nope, query_rope, new_latent, new_rope, key_absorb, value_up):
    decode_order = jnp.argsort(target_shard, stable=True)
    latent_decode = latent_cache[decode_order]
    rope_decode = rope_cache[decode_order]
    token_request = request_of(jnp.arange(TOKENS, dtype=jnp.int32), lengths)
    query_latent = jnp.einsum('srhn,hnl->srhl', query_nope.astype(jnp.float32), key_absorb.astype(jnp.float32)).astype(jnp.bfloat16)
    score_scale = 1.0 / math.sqrt(D_NOPE + D_ROPE)
    row_request = jnp.arange(REQS * HEADS, dtype=jnp.int32) // HEADS
    key_latent = jnp.concatenate([latent_cache, new_latent.reshape(STEPS * REQS, D_LAT)], axis=0)
    key_rope = jnp.concatenate([rope_cache, new_rope.reshape(STEPS * REQS, D_ROPE)], axis=0)
    fresh_index = jnp.arange(STEPS * REQS, dtype=jnp.int32)
    key_request = jnp.concatenate([token_request, fresh_index % REQS])
    key_step = jnp.concatenate([jnp.zeros((TOKENS,), jnp.int32), fresh_index // REQS])
    results = []
    for step_now in range(STEPS):
        lat_rows = query_latent[step_now].reshape(REQS * HEADS, D_LAT)
        rope_rows = query_rope[step_now].reshape(REQS * HEADS, D_ROPE)
        usable = (key_request[None, :] == row_request[:, None]) & (key_step[None, :] <= step_now)
        scores = (jnp.dot(lat_rows, key_latent.T, preferred_element_type=jnp.float32) + jnp.dot(rope_rows, key_rope.T, preferred_element_type=jnp.float32)) * score_scale
        masked = jnp.where(usable, scores, NEG)
        row_peak = lax.optimization_barrier(jnp.max(masked, axis=-1))
        weights = jnp.where(usable, jnp.exp(masked - row_peak[:, None]), 0.0)
        totals = lax.optimization_barrier(jnp.sum(weights, axis=-1))
        weighted = jnp.dot(weights.astype(jnp.bfloat16), key_latent, preferred_element_type=jnp.float32)
        latent_out = (weighted / totals[:, None]).astype(jnp.bfloat16).reshape(REQS, HEADS, D_LAT)
        results.append(jnp.einsum('rhl,hlv->rhv', latent_out.astype(jnp.float32), value_up.astype(jnp.float32)).astype(jnp.bfloat16))
    return (jnp.stack(results), latent_decode, rope_decode)
```

```python
import functools
import math

import jax
import jax.numpy as jnp
from jax import lax
from jax.experimental import pallas as pl
from jax.experimental.pallas import tpu as pltpu
from jax.sharding import PartitionSpec as P

NEG = -1e30
NX = 4
NZ = 8
CTX = NX * NZ
PER = 56
MSG = 64
LAT = 512
ROPE = 64
TOK = PER * CTX
HALF = 384
F32 = jnp.float32
BF16 = jnp.bfloat16
MESH = pl.DeviceIdType.MESH


def iota(shape, dim):
    return lax.broadcasted_iota(jnp.int32, shape, dim)


def pieces(column):
    first = column.astype(BF16).astype(F32)
    rest = column - first
    second = rest.astype(BF16).astype(F32)
    return first, second, rest - second


def pack_part(num, peak, den):
    rows = num.shape[0]
    lane = iota((rows, 128), 1)
    stats = jnp.zeros((rows, 128), F32)
    for at, column in enumerate(pieces(peak) + pieces(den)):
        stats = jnp.where(lane == at, column, stats)
    low = jnp.concatenate([num[:, HALF:], stats, jnp.zeros((rows, 128), F32)], axis=1)
    top = num[:, :HALF].reshape(rows // 8, 8, HALF)
    low = low.reshape(rows // 8, 8, HALF)
    return jnp.concatenate([top, low], axis=1).astype(BF16)


def halves(message):
    n = message.shape[0]
    value = message.astype(F32)
    top = value[:, :8, :].reshape(n * 8, HALF)
    low = value[:, 8:, :].reshape(n * 8, HALF)
    return top, low


def unpack_part(message):
    top, low = halves(message)
    num = jnp.concatenate([top, low[:, :128]], axis=1)
    peak = low[:, 128:129] + low[:, 129:130] + low[:, 130:131]
    den = low[:, 131:132] + low[:, 132:133] + low[:, 133:134]
    return num, peak, den


def join_parts(parts):
    peak = functools.reduce(jnp.maximum, [p[1] for p in parts])
    num = den = 0.0
    for one in parts:
        factor = jnp.exp(one[1] - peak)
        num = num + one[0] * factor
        den = den + one[2] * factor
    return num, peak, den


def exchange_kernel(
    scale,
    len_ref, tgt_ref, qn_ref, qr_ref, nl_ref, nr_ref, ka_ref, vu_ref, lat_hbm, rope_hbm,
    land_ref, att_ref,
    lat, rope, rope_t, pos, outbox, qz, qx, ql_s, qr_s, sc, wb, ca_src, ca_dst, cb_src, cb_dst,
    in_sem, own_sem, send_sem, recv_sem, qa_s, qa_r, qb_s, qb_r, ca_s, ca_r, cb_s, cb_r,
):
    me = lax.axis_index("ctx")
    z = me // NX
    x = lax.rem(me, NX)

    def along_z(k):
        return lax.rem(z + k, NZ)

    def along_x(k):
        return lax.rem(x + k, NX)

    load_lat = pltpu.make_async_copy(lat_hbm, lat, in_sem.at[0])
    load_rope = pltpu.make_async_copy(rope_hbm, rope, in_sem.at[1])
    load_lat.start()
    load_rope.start()

    barrier = pltpu.get_barrier_semaphore()

    def greet(i, carry):
        pl.semaphore_signal(
            barrier, inc=1, device_id={"ctx": lax.rem(me + i, CTX)}, device_id_type=MESH
        )
        return carry

    lax.fori_loop(1, CTX, greet, 0)

    qn = qn_ref[...]
    row8 = iota((8, LAT), 0)
    ql = jnp.where(
        lax.rem(row8, 2) == 0,
        jnp.dot(qn, ka_ref[0], preferred_element_type=F32),
        jnp.dot(qn, ka_ref[1], preferred_element_type=F32),
    )
    ql = ql.astype(BF16).astype(F32)
    qr = jnp.concatenate([qr_ref[...].astype(F32), jnp.zeros((8, 256 - ROPE), F32)], axis=1)
    own_query = jnp.concatenate(
        [ql[:, :HALF], jnp.concatenate([ql[:, HALF:], qr], axis=1)], axis=0
    ).astype(BF16)
    qz[z] = own_query

    shard = iota((CTX, 128), 0)
    hot = [(tgt_ref[b : b + 1, :] == shard).astype(F32) for b in range(TOK // 128)]
    before = (iota((128, 128), 0) < iota((128, 128), 1)).astype(BF16)
    prefix = jnp.dot(
        jnp.concatenate(hot, axis=0).astype(BF16), before, preferred_element_type=F32
    )
    base = (MSG * shard).astype(F32)
    for b in range(TOK // 128):
        part = hot[b]
        place = jnp.sum(part * (prefix[CTX * b : CTX * (b + 1)] + base), axis=0, keepdims=True)
        pos[0:1, 128 * b : 128 * (b + 1)] = place.astype(jnp.int32)
        base = base + jnp.sum(part, axis=1, keepdims=True)

    load_rope.wait()
    rope_t[...] = jnp.transpose(rope[...].astype(F32)).astype(BF16)
    load_lat.wait()

    def group_z(i):
        half = (i + 1) // 2
        return along_z(4 + half * (1 - 2 * lax.rem(i, 2)))

    rows = NX * MSG

    def build(i):
        first = pl.multiple_of(group_z(i) * rows, rows)
        one_hot = (pos[0:1, :] - first == iota((rows, TOK), 0)).astype(F32).astype(BF16)
        moved = jnp.dot(one_hot, lat[...], preferred_element_type=F32)
        turned = jnp.dot(one_hot, rope_t[...], preferred_element_type=F32)
        for j in range(NX):
            block = turned[MSG * j : MSG * (j + 1)]
            packed = jnp.concatenate([block[8 * k : 8 * (k + 1)] for k in range(8)], axis=1)
            whole = jnp.concatenate([moved[MSG * j : MSG * j + PER], packed], axis=0)
            outbox[pl.ds(first + MSG * j, MSG), :] = whole.astype(BF16)

    def message(i, k):
        there = group_z(i) * NX + along_x(k)
        return pltpu.make_async_remote_copy(
            src_ref=outbox.at[pl.ds(pl.multiple_of(there * MSG, MSG), MSG)],
            dst_ref=land_ref.at[pl.ds(pl.multiple_of(me * MSG, MSG), MSG)],
            send_sem=send_sem.at[there],
            recv_sem=recv_sem.at[me],
            device_id={"ctx": there},
            device_id_type=MESH,
        )

    def send(i, low=0):
        for k in range(low, NX):
            message(i, k).start()

    def build_send(i, carry):
        build(i)
        send(i)
        return carry

    def build_only(i, carry):
        build(i)
        return carry

    build(jnp.int32(0))
    pl.semaphore_wait(barrier, CTX - 1)

    def spread_z(src, dst, s_sem, r_sem, k, own):
        there = along_z(k)
        return pltpu.make_async_remote_copy(
            src_ref=src.at[z if own else there],
            dst_ref=dst.at[z],
            send_sem=s_sem.at[k],
            recv_sem=r_sem.at[k],
            device_id={"ctx": there * NX + x},
            device_id_type=MESH,
        )

    def spread_x(src, dst, s_sem, r_sem, k, own):
        there = along_x(k)
        return pltpu.make_async_remote_copy(
            src_ref=src if own else src.at[there],
            dst_ref=dst.at[x],
            send_sem=s_sem.at[k],
            recv_sem=r_sem.at[k],
            device_id={"ctx": z * NX + there},
            device_id_type=MESH,
        )

    def arrive_z(dst, r_sem, s_sem, k):
        return pltpu.make_async_remote_copy(
            src_ref=dst.at[z],
            dst_ref=dst.at[along_z(NZ - k)],
            send_sem=s_sem.at[k],
            recv_sem=r_sem.at[k],
            device_id={"ctx": along_z(k) * NX + x},
            device_id_type=MESH,
        )

    def arrive_x(dst, r_sem, s_sem, k):
        return pltpu.make_async_remote_copy(
            src_ref=dst.at[x],
            dst_ref=dst.at[along_x(NX - k)],
            send_sem=s_sem.at[k],
            recv_sem=r_sem.at[k],
            device_id={"ctx": z * NX + along_x(k)},
            device_id_type=MESH,
        )

    for k in range(1, NZ):
        spread_z(qz, qz, qa_s, qa_r, k, True).start()
    send(jnp.int32(0))
    lax.fori_loop(1, 3, build_send, 0)

    for k in range(1, NZ):
        arrive_z(qz, qa_r, qa_s, k).wait_recv()
    for k in range(1, NX):
        spread_x(qz, qx, qb_s, qb_r, k, True).start()
    qx[x] = qz[...]
    lax.fori_loop(3, 5, build_send, 0)
    lax.fori_loop(5, 8, build_only, 0)
    for k in range(1, NX):
        arrive_x(qx, qb_r, qb_s, k).wait_recv()

    for s in range(NX):
        top, low = halves(qx[s])
        ql_s[64 * s : 64 * (s + 1), :] = jnp.concatenate([top, low[:, :128]], axis=1).astype(BF16)
        qr_s[64 * s : 64 * (s + 1), :] = low[:, 128 : 128 + ROPE].astype(BF16)
    heads = 8 * CTX
    chunk = 256
    bound = len_ref[0] - me * TOK
    row_request = lax.rem(iota((heads, chunk), 0) // 2, 2)
    peak = jnp.full((heads, 1), NEG, F32)
    for c in range(TOK // chunk):
        at = slice(chunk * c, chunk * (c + 1))
        scores = lax.dot_general(
            ql_s[...], lat[at, :], (((1,), (1,)), ((), ())), preferred_element_type=F32
        ) + jnp.dot(qr_s[...], rope[:, at], preferred_element_type=F32)
        token_request = (iota((heads, chunk), 1) + chunk * c >= bound).astype(jnp.int32)
        scores = jnp.where(token_request == row_request, scores * scale, NEG)
        sc[:, at] = scores
        peak = jnp.maximum(peak, jnp.max(scores, axis=1, keepdims=True))
    den = jnp.zeros((heads, 1), F32)
    for c in range(TOK // chunk):
        at = slice(chunk * c, chunk * (c + 1))
        scores = sc[:, at]
        weight = jnp.where(scores > 0.5 * NEG, jnp.exp(scores - peak), 0.0)
        den = den + jnp.sum(weight, axis=1, keepdims=True)
        wb[:, at] = weight.astype(BF16)
    num = jnp.dot(wb[...], lat[...], preferred_element_type=F32)
    for s in range(NX):
        at = slice(64 * s, 64 * (s + 1))
        ca_src[s] = pack_part(num[at], peak[at], den[at])

    for k in range(1, NX):
        spread_x(ca_src, ca_dst, ca_s, ca_r, k, False).start()
    ca_dst[x] = ca_src[x]
    send(jnp.int32(5))
    send(jnp.int32(6))

    for k in range(1, NX):
        arrive_x(ca_dst, ca_r, ca_s, k).wait_recv()
    cb_src[...] = pack_part(*join_parts([unpack_part(ca_dst[s]) for s in range(NX)]))
    for k in range(1, NZ):
        spread_z(cb_src, cb_dst, cb_s, cb_r, k, False).start()
    cb_dst[z] = cb_src[z]
    send(jnp.int32(7), 1)
    mine = pl.ds(pl.multiple_of(me * MSG, MSG), MSG)
    keep = pltpu.make_async_copy(outbox.at[mine], land_ref.at[mine], own_sem)
    keep.start()

    top, low = halves(qz[pl.ds(z, 1)])
    own_ql = jnp.concatenate([top, low[:, :128]], axis=1)
    own_qr = low[:, 128 : 128 + ROPE]
    row_at = iota((8, 1), 0)
    fresh = []
    for f in range(4):
        key_latent = nl_ref[f : f + 1, :].astype(F32)
        key_rope = nr_ref[f : f + 1, :].astype(F32)
        score = (
            jnp.sum(own_ql * key_latent, axis=1, keepdims=True)
            + jnp.sum(own_qr * key_rope, axis=1, keepdims=True)
        ) * scale
        usable = (f // 2 <= row_at // 4) & (f % 2 == lax.rem(row_at // 2, 2))
        fresh.append((usable, jnp.where(usable, score, NEG), key_latent))

    for k in range(1, NZ):
        arrive_z(cb_dst, cb_r, cb_s, k).wait_recv()
    num, peak, den = join_parts([unpack_part(cb_dst[pl.ds(s, 1)]) for s in range(NZ)])
    top_peak = functools.reduce(jnp.maximum, [one[1] for one in fresh], peak)
    factor = jnp.exp(peak - top_peak)
    num = num * factor
    den = den * factor
    for usable, score, key_latent in fresh:
        weight = jnp.where(usable, jnp.exp(score - top_peak), 0.0)
        den = den + weight
        num = num + weight.astype(BF16).astype(F32) * key_latent
    latent_out = (num / den).astype(BF16)
    att_ref[...] = jnp.where(
        lax.rem(iota((8, 128), 0), 2) == 0,
        jnp.dot(latent_out, vu_ref[0], preferred_element_type=F32),
        jnp.dot(latent_out, vu_ref[1], preferred_element_type=F32),
    ).astype(BF16)

    def settle(i, carry):
        there = lax.rem(me + i, CTX)
        one = pltpu.make_async_remote_copy(
            src_ref=outbox.at[pl.ds(pl.multiple_of(there * MSG, MSG), MSG)],
            dst_ref=land_ref.at[pl.ds(pl.multiple_of(there * MSG, MSG), MSG)],
            send_sem=send_sem.at[there],
            recv_sem=recv_sem.at[there],
            device_id={"ctx": there},
            device_id_type=MESH,
        )
        one.wait_send()
        one.wait_recv()
        return carry

    lax.fori_loop(1, CTX, settle, 0)
    keep.wait()
    for k in range(1, NZ):
        spread_z(qz, qz, qa_s, qa_r, k, True).wait_send()
        spread_z(cb_src, cb_dst, cb_s, cb_r, k, False).wait_send()
    for k in range(1, NX):
        spread_x(qz, qx, qb_s, qb_r, k, True).wait_send()
        spread_x(ca_src, ca_dst, ca_s, ca_r, k, False).wait_send()


def unpack_kernel(land_ref, lat_ref, rope_ref):
    turned = []
    for s in range(0, land_ref.shape[0] // MSG, 2):
        both = []
        for at in (MSG * s, MSG * (s + 1)):
            value = land_ref[at : at + MSG, :].astype(F32)
            both.append(value[:PER])
            packed = value[PER:]
            turned += [packed[:, ROPE * k : ROPE * (k + 1)] for k in range(PER // 8)]
        lat_ref[PER * s : PER * (s + 2), :] = jnp.concatenate(both, axis=0).astype(BF16)
    rope_ref[...] = jnp.transpose(jnp.concatenate(turned, axis=0)).astype(BF16)


def local(
    latent_cache,
    rope_cache,
    lengths,
    target_shard,
    query_nope,
    query_rope,
    new_latent,
    new_rope,
    key_absorb,
    value_up,
):
    scale = 1.0 / math.sqrt(query_nope.shape[3] + ROPE)
    vmem = pl.BlockSpec(memory_space=pltpu.VMEM)
    anywhere = pl.BlockSpec(memory_space=pl.ANY)
    dma = pltpu.SemaphoreType.DMA
    land, attention = pl.pallas_call(
        functools.partial(exchange_kernel, scale),
        out_shape=(
            jax.ShapeDtypeStruct((CTX * MSG, LAT), BF16),
            jax.ShapeDtypeStruct((8, 128), BF16),
        ),
        in_specs=[pl.BlockSpec(memory_space=pltpu.SMEM)] + [vmem] * 7 + [anywhere] * 2,
        out_specs=(anywhere, vmem),
        scratch_shapes=[
            pltpu.VMEM((TOK, LAT), BF16),
            pltpu.VMEM((ROPE, TOK), BF16),
            pltpu.VMEM((TOK, ROPE), BF16),
            pltpu.VMEM((8, TOK), jnp.int32),
            pltpu.VMEM((CTX * MSG, LAT), BF16),
            pltpu.VMEM((NZ, 16, HALF), BF16),
            pltpu.VMEM((NX, NZ, 16, HALF), BF16),
            pltpu.VMEM((8 * CTX, LAT), BF16),
            pltpu.VMEM((8 * CTX, ROPE), BF16),
            pltpu.VMEM((8 * CTX, TOK), F32),
            pltpu.VMEM((8 * CTX, TOK), BF16),
            pltpu.VMEM((NX, NZ, 16, HALF), BF16),
            pltpu.VMEM((NX, NZ, 16, HALF), BF16),
            pltpu.VMEM((NZ, 16, HALF), BF16),
            pltpu.VMEM((NZ, 16, HALF), BF16),
            dma((2,)),
            dma,
            dma((CTX,)),
            dma((CTX,)),
            dma((NZ,)),
            dma((NZ,)),
            dma((NX,)),
            dma((NX,)),
            dma((NX,)),
            dma((NX,)),
            dma((NZ,)),
            dma((NZ,)),
        ],
        name="exchange",
        compiler_params=pltpu.CompilerParams(
            collective_id=1, has_side_effects=True, vmem_limit_bytes=40 << 20
        ),
    )(
        lengths,
        target_shard.reshape(TOK // 128, 128),
        query_nope.reshape(8, 128),
        query_rope.reshape(8, ROPE),
        new_latent.reshape(4, LAT),
        new_rope.reshape(4, ROPE),
        key_absorb,
        value_up,
        latent_cache,
        rope_cache.T,
    )
    latent_decode, rope_decode = pl.pallas_call(
        unpack_kernel,
        grid=(2,),
        out_shape=(
            jax.ShapeDtypeStruct((TOK, LAT), BF16),
            jax.ShapeDtypeStruct((ROPE, TOK), BF16),
        ),
        in_specs=[pl.BlockSpec((CTX * MSG // 2, LAT), lambda i: (i, 0))],
        out_specs=(
            pl.BlockSpec((TOK // 2, LAT), lambda i: (i, 0)),
            pl.BlockSpec((ROPE, TOK // 2), lambda i: (0, i)),
        ),
        name="unpack",
        compiler_params=pltpu.CompilerParams(vmem_limit_bytes=40 << 20),
    )(land)
    return attention.reshape(query_nope.shape), latent_decode, rope_decode.T


def solution(mesh):
    placed = (
        P(("req", "ctx"), None),
        P(("req", "ctx"), None),
        P("req"),
        P(("req", "ctx")),
        P(None, "req", "ctx", None),
        P(None, "req", "ctx", None),
        P(None, "req", None),
        P(None, "req", None),
        P("ctx", None, None),
        P("ctx", None, None),
    )
    return jax.shard_map(
        local,
        mesh=mesh,
        in_specs=placed,
        out_specs=(P(None, "req", "ctx", None), P(("req", "ctx"), None), P(("req", "ctx"), None)),
        check_vma=False,
    )
```

```python
import functools
import math

import jax
import jax.numpy as jnp
from jax import lax
from jax.experimental import pallas as pl
from jax.experimental.pallas import tpu as pltpu
from jax.sharding import PartitionSpec as P

NEG = -1e30
NX = 4
NZ = 8
CTX = NX * NZ
PER = 56
MSG = 64
LAT = 512
ROPE = 64
TOK = PER * CTX
HALF = 384
F32 = jnp.float32
BF16 = jnp.bfloat16
MESH = pl.DeviceIdType.MESH


def iota(shape, dim):
    return lax.broadcasted_iota(jnp.int32, shape, dim)


def pieces(column):
    first = column.astype(BF16).astype(F32)
    rest = column - first
    second = rest.astype(BF16).astype(F32)
    return first, second, rest - second


def pack_part(num, peak, den):
    rows = num.shape[0]
    lane = iota((rows, 128), 1)
    stats = jnp.zeros((rows, 128), F32)
    for at, column in enumerate(pieces(peak) + pieces(den)):
        stats = jnp.where(lane == at, column, stats)
    low = jnp.concatenate([num[:, HALF:], stats, jnp.zeros((rows, 128), F32)], axis=1)
    top = num[:, :HALF].reshape(rows // 8, 8, HALF)
    low = low.reshape(rows // 8, 8, HALF)
    return jnp.concatenate([top, low], axis=1).astype(BF16)


def halves(message):
    n = message.shape[0]
    value = message.astype(F32)
    top = value[:, :8, :].reshape(n * 8, HALF)
    low = value[:, 8:, :].reshape(n * 8, HALF)
    return top, low


def unpack_part(message):
    top, low = halves(message)
    num = jnp.concatenate([top, low[:, :128]], axis=1)
    peak = low[:, 128:129] + low[:, 129:130] + low[:, 130:131]
    den = low[:, 131:132] + low[:, 132:133] + low[:, 133:134]
    return num, peak, den


def join_parts(parts):
    peak = functools.reduce(jnp.maximum, [p[1] for p in parts])
    num = den = 0.0
    for one in parts:
        factor = jnp.exp(one[1] - peak)
        num = num + one[0] * factor
        den = den + one[2] * factor
    return num, peak, den


def exchange_kernel(
    scale,
    tgt_hbm, ka_hbm, qn_hbm, qr_hbm, rope_hbm, lat_hbm, len_hbm, nl_hbm, nr_hbm, vu_hbm,
    land_ref, att_ref,
    tgt_ref, ka_ref, qn_ref, qr_ref, rope, lat, len_ref, nl_ref, nr_ref, vu_ref, rope_t, pos, outbox, qz, qx, ql_s, qr_s, sc, wb, ca_src, ca_dst, cb_src, cb_dst,
    in_sem, own_sem, send_sem, recv_sem, qa_s, qa_r, qb_s, qb_r, ca_s, ca_r, cb_s, cb_r,
):
    me = lax.axis_index("ctx")
    z = me // NX
    x = lax.rem(me, NX)

    def along_z(k):
        return lax.rem(z + k, NZ)

    def along_x(k):
        return lax.rem(x + k, NX)

    loads = [
        pltpu.make_async_copy(src, dst, in_sem.at[i])
        for i, (src, dst) in enumerate(
            (
                (tgt_hbm, tgt_ref),
                (ka_hbm, ka_ref),
                (qn_hbm, qn_ref),
                (qr_hbm, qr_ref),
                (rope_hbm, rope),
                (lat_hbm, lat),
                (len_hbm, len_ref),
                (nl_hbm, nl_ref),
                (nr_hbm, nr_ref),
                (vu_hbm, vu_ref),
            )
        )
    ]
    for load in loads:
        load.start()

    barrier = pltpu.get_barrier_semaphore()

    def greet(i, carry):
        pl.semaphore_signal(
            barrier, inc=1, device_id={"ctx": lax.rem(me + i, CTX)}, device_id_type=MESH
        )
        return carry

    lax.fori_loop(1, CTX, greet, 0)

    for load in loads[1:4]:
        load.wait()
    qn = qn_ref[...]
    row8 = iota((8, LAT), 0)
    ql = jnp.where(
        lax.rem(row8, 2) == 0,
        jnp.dot(qn, ka_ref[0], preferred_element_type=F32),
        jnp.dot(qn, ka_ref[1], preferred_element_type=F32),
    )
    ql = ql.astype(BF16).astype(F32)
    qr = jnp.concatenate([qr_ref[...].astype(F32), jnp.zeros((8, 256 - ROPE), F32)], axis=1)
    own_query = jnp.concatenate(
        [ql[:, :HALF], jnp.concatenate([ql[:, HALF:], qr], axis=1)], axis=0
    ).astype(BF16)
    qz[z] = own_query

    loads[0].wait()
    shard = iota((CTX, 128), 0)
    hot = [(tgt_ref[b : b + 1, :] == shard).astype(F32) for b in range(TOK // 128)]
    before = (iota((128, 128), 0) < iota((128, 128), 1)).astype(BF16)
    prefix = jnp.dot(
        jnp.concatenate(hot, axis=0).astype(BF16), before, preferred_element_type=F32
    )
    base = (MSG * shard).astype(F32)
    for b in range(TOK // 128):
        part = hot[b]
        place = jnp.sum(part * (prefix[CTX * b : CTX * (b + 1)] + base), axis=0, keepdims=True)
        pos[0:1, 128 * b : 128 * (b + 1)] = place.astype(jnp.int32)
        base = base + jnp.sum(part, axis=1, keepdims=True)

    loads[4].wait()
    rope_t[...] = jnp.transpose(rope[...].astype(F32)).astype(BF16)
    loads[5].wait()

    def group_z(i):
        half = (i + 1) // 2
        return along_z(4 + half * (1 - 2 * lax.rem(i, 2)))

    rows = NX * MSG

    def build(i):
        first = pl.multiple_of(group_z(i) * rows, rows)
        one_hot = (pos[0:1, :] - first == iota((rows, TOK), 0)).astype(F32).astype(BF16)
        moved = jnp.dot(one_hot, lat[...], preferred_element_type=F32)
        turned = jnp.dot(one_hot, rope_t[...], preferred_element_type=F32)
        for j in range(NX):
            block = turned[MSG * j : MSG * (j + 1)]
            packed = jnp.concatenate([block[8 * k : 8 * (k + 1)] for k in range(8)], axis=1)
            whole = jnp.concatenate([moved[MSG * j : MSG * j + PER], packed], axis=0)
            outbox[pl.ds(first + MSG * j, MSG), :] = whole.astype(BF16)

    def message(i, k):
        there = group_z(i) * NX + along_x(k)
        return pltpu.make_async_remote_copy(
            src_ref=outbox.at[pl.ds(pl.multiple_of(there * MSG, MSG), MSG)],
            dst_ref=land_ref.at[pl.ds(pl.multiple_of(me * MSG, MSG), MSG)],
            send_sem=send_sem.at[there],
            recv_sem=recv_sem.at[me],
            device_id={"ctx": there},
            device_id_type=MESH,
        )

    def send(i, low=0):
        for k in range(low, NX):
            message(i, k).start()

    def build_send(i, carry):
        build(i)
        send(i)
        return carry

    def build_only(i, carry):
        build(i)
        return carry

    build(jnp.int32(0))
    pl.semaphore_wait(barrier, CTX - 1)

    def spread_z(src, dst, s_sem, r_sem, k, own):
        there = along_z(k)
        return pltpu.make_async_remote_copy(
            src_ref=src.at[z if own else there],
            dst_ref=dst.at[z],
            send_sem=s_sem.at[k],
            recv_sem=r_sem.at[k],
            device_id={"ctx": there * NX + x},
            device_id_type=MESH,
        )

    def spread_x(src, dst, s_sem, r_sem, k, own):
        there = along_x(k)
        return pltpu.make_async_remote_copy(
            src_ref=src if own else src.at[there],
            dst_ref=dst.at[x],
            send_sem=s_sem.at[k],
            recv_sem=r_sem.at[k],
            device_id={"ctx": z * NX + there},
            device_id_type=MESH,
        )

    def arrive_z(dst, r_sem, s_sem, k):
        return pltpu.make_async_remote_copy(
            src_ref=dst.at[z],
            dst_ref=dst.at[along_z(NZ - k)],
            send_sem=s_sem.at[k],
            recv_sem=r_sem.at[k],
            device_id={"ctx": along_z(k) * NX + x},
            device_id_type=MESH,
        )

    def arrive_x(dst, r_sem, s_sem, k):
        return pltpu.make_async_remote_copy(
            src_ref=dst.at[x],
            dst_ref=dst.at[along_x(NX - k)],
            send_sem=s_sem.at[k],
            recv_sem=r_sem.at[k],
            device_id={"ctx": z * NX + along_x(k)},
            device_id_type=MESH,
        )

    for k in range(1, NZ):
        spread_z(qz, qz, qa_s, qa_r, k, True).start()
    send(jnp.int32(0))
    lax.fori_loop(1, 3, build_send, 0)

    for k in range(1, NZ):
        arrive_z(qz, qa_r, qa_s, k).wait_recv()
    for k in range(1, NX):
        spread_x(qz, qx, qb_s, qb_r, k, True).start()
    qx[x] = qz[...]
    lax.fori_loop(3, 5, build_send, 0)
    lax.fori_loop(5, 8, build_only, 0)
    for k in range(1, NX):
        arrive_x(qx, qb_r, qb_s, k).wait_recv()

    for s in range(NX):
        top, low = halves(qx[s])
        ql_s[64 * s : 64 * (s + 1), :] = jnp.concatenate([top, low[:, :128]], axis=1).astype(BF16)
        qr_s[64 * s : 64 * (s + 1), :] = low[:, 128 : 128 + ROPE].astype(BF16)
    heads = 8 * CTX
    chunk = 256
    loads[6].wait()
    bound = len_ref[0] - me * TOK
    row_request = lax.rem(iota((heads, chunk), 0) // 2, 2)
    peak = jnp.full((heads, 1), NEG, F32)
    for c in range(TOK // chunk):
        at = slice(chunk * c, chunk * (c + 1))
        scores = lax.dot_general(
            ql_s[...], lat[at, :], (((1,), (1,)), ((), ())), preferred_element_type=F32
        ) + jnp.dot(qr_s[...], rope[:, at], preferred_element_type=F32)
        token_request = (iota((heads, chunk), 1) + chunk * c >= bound).astype(jnp.int32)
        scores = jnp.where(token_request == row_request, scores * scale, NEG)
        sc[:, at] = scores
        peak = jnp.maximum(peak, jnp.max(scores, axis=1, keepdims=True))
    den = jnp.zeros((heads, 1), F32)
    for c in range(TOK // chunk):
        at = slice(chunk * c, chunk * (c + 1))
        scores = sc[:, at]
        weight = jnp.where(scores > 0.5 * NEG, jnp.exp(scores - peak), 0.0)
        den = den + jnp.sum(weight, axis=1, keepdims=True)
        wb[:, at] = weight.astype(BF16)
    num = jnp.dot(wb[...], lat[...], preferred_element_type=F32)
    for s in range(NX):
        at = slice(64 * s, 64 * (s + 1))
        ca_src[s] = pack_part(num[at], peak[at], den[at])

    for k in range(1, NX):
        spread_x(ca_src, ca_dst, ca_s, ca_r, k, False).start()
    ca_dst[x] = ca_src[x]
    send(jnp.int32(5))
    send(jnp.int32(6))

    for k in range(1, NX):
        arrive_x(ca_dst, ca_r, ca_s, k).wait_recv()
    cb_src[...] = pack_part(*join_parts([unpack_part(ca_dst[s]) for s in range(NX)]))
    for k in range(1, NZ):
        spread_z(cb_src, cb_dst, cb_s, cb_r, k, False).start()
    cb_dst[z] = cb_src[z]
    send(jnp.int32(7), 1)
    mine = pl.ds(pl.multiple_of(me * MSG, MSG), MSG)
    keep = pltpu.make_async_copy(outbox.at[mine], land_ref.at[mine], own_sem)
    keep.start()

    top, low = halves(qz[pl.ds(z, 1)])
    own_ql = jnp.concatenate([top, low[:, :128]], axis=1)
    own_qr = low[:, 128 : 128 + ROPE]
    row_at = iota((8, 1), 0)
    fresh = []
    for load in loads[7:]:
        load.wait()
    for f in range(4):
        key_latent = nl_ref[f // 2].astype(F32)[f % 2 : f % 2 + 1, :]
        key_rope = nr_ref[f // 2].astype(F32)[f % 2 : f % 2 + 1, :]
        score = (
            jnp.sum(own_ql * key_latent, axis=1, keepdims=True)
            + jnp.sum(own_qr * key_rope, axis=1, keepdims=True)
        ) * scale
        usable = (f // 2 <= row_at // 4) & (f % 2 == lax.rem(row_at // 2, 2))
        fresh.append((usable, jnp.where(usable, score, NEG), key_latent))

    for k in range(1, NZ):
        arrive_z(cb_dst, cb_r, cb_s, k).wait_recv()
    num, peak, den = join_parts([unpack_part(cb_dst[pl.ds(s, 1)]) for s in range(NZ)])
    top_peak = functools.reduce(jnp.maximum, [one[1] for one in fresh], peak)
    factor = jnp.exp(peak - top_peak)
    num = num * factor
    den = den * factor
    for usable, score, key_latent in fresh:
        weight = jnp.where(usable, jnp.exp(score - top_peak), 0.0)
        den = den + weight
        num = num + weight.astype(BF16).astype(F32) * key_latent
    latent_out = (num / den).astype(BF16)
    att_ref[...] = jnp.where(
        lax.rem(iota((8, 128), 0), 2) == 0,
        jnp.dot(latent_out, vu_ref[0], preferred_element_type=F32),
        jnp.dot(latent_out, vu_ref[1], preferred_element_type=F32),
    ).astype(BF16)

    def settle(i, carry):
        there = lax.rem(me + i, CTX)
        one = pltpu.make_async_remote_copy(
            src_ref=outbox.at[pl.ds(pl.multiple_of(there * MSG, MSG), MSG)],
            dst_ref=land_ref.at[pl.ds(pl.multiple_of(there * MSG, MSG), MSG)],
            send_sem=send_sem.at[there],
            recv_sem=recv_sem.at[there],
            device_id={"ctx": there},
            device_id_type=MESH,
        )
        one.wait_send()
        one.wait_recv()
        return carry

    lax.fori_loop(1, CTX, settle, 0)
    keep.wait()
    for k in range(1, NZ):
        spread_z(qz, qz, qa_s, qa_r, k, True).wait_send()
        spread_z(cb_src, cb_dst, cb_s, cb_r, k, False).wait_send()
    for k in range(1, NX):
        spread_x(qz, qx, qb_s, qb_r, k, True).wait_send()
        spread_x(ca_src, ca_dst, ca_s, ca_r, k, False).wait_send()


def unpack_kernel(land_ref, part_ref, lat_ref, rope_ref, att_ref):
    att_ref[...] = part_ref[...]
    turned = []
    for s in range(0, land_ref.shape[0] // MSG, 2):
        both = []
        for at in (MSG * s, MSG * (s + 1)):
            value = land_ref[at : at + MSG, :].astype(F32)
            both.append(value[:PER])
            packed = value[PER:]
            turned += [packed[:, ROPE * k : ROPE * (k + 1)] for k in range(PER // 8)]
        lat_ref[PER * s : PER * (s + 2), :] = jnp.concatenate(both, axis=0).astype(BF16)
    rope_ref[...] = jnp.transpose(jnp.concatenate(turned, axis=0)).astype(BF16)


def local(
    latent_cache,
    rope_cache,
    lengths,
    target_shard,
    query_nope,
    query_rope,
    new_latent,
    new_rope,
    key_absorb,
    value_up,
):
    scale = 1.0 / math.sqrt(query_nope.shape[3] + ROPE)
    vmem = pl.BlockSpec(memory_space=pltpu.VMEM)
    hbm = pl.BlockSpec(memory_space=pltpu.HBM)
    anywhere = pl.BlockSpec(memory_space=pl.ANY)
    dma = pltpu.SemaphoreType.DMA
    land, attention = pl.pallas_call(
        functools.partial(exchange_kernel, scale),
        out_shape=(
            pltpu.VMEM((CTX * MSG, LAT), BF16),
            pltpu.VMEM((8, 128), BF16),
        ),
        in_specs=[hbm] * 10,
        out_specs=(anywhere, vmem),
        scratch_shapes=[
            pltpu.VMEM((TOK // 128, 128), jnp.int32),
            pltpu.VMEM(key_absorb.shape, BF16),
            pltpu.VMEM((8, 128), BF16),
            pltpu.VMEM((8, ROPE), BF16),
            pltpu.VMEM((ROPE, TOK), BF16),
            pltpu.VMEM((TOK, LAT), BF16),
            pltpu.SMEM((2,), jnp.int32),
            pltpu.VMEM(new_latent.shape, BF16),
            pltpu.VMEM(new_rope.shape, BF16),
            pltpu.VMEM(value_up.shape, BF16),
            pltpu.VMEM((TOK, ROPE), BF16),
            pltpu.VMEM((8, TOK), jnp.int32),
            pltpu.VMEM((CTX * MSG, LAT), BF16),
            pltpu.VMEM((NZ, 16, HALF), BF16),
            pltpu.VMEM((NX, NZ, 16, HALF), BF16),
            pltpu.VMEM((8 * CTX, LAT), BF16),
            pltpu.VMEM((8 * CTX, ROPE), BF16),
            pltpu.VMEM((8 * CTX, TOK), F32),
            pltpu.VMEM((8 * CTX, TOK), BF16),
            pltpu.VMEM((NX, NZ, 16, HALF), BF16),
            pltpu.VMEM((NX, NZ, 16, HALF), BF16),
            pltpu.VMEM((NZ, 16, HALF), BF16),
            pltpu.VMEM((NZ, 16, HALF), BF16),
            dma((10,)),
            dma,
            dma((CTX,)),
            dma((CTX,)),
            dma((NZ,)),
            dma((NZ,)),
            dma((NX,)),
            dma((NX,)),
            dma((NX,)),
            dma((NX,)),
            dma((NZ,)),
            dma((NZ,)),
        ],
        name="exchange",
        compiler_params=pltpu.CompilerParams(
            collective_id=1, has_side_effects=True, vmem_limit_bytes=40 << 20
        ),
    )(
        *(pltpu.with_memory_space_constraint(array, pltpu.HBM) for array in (
            target_shard.reshape(TOK // 128, 128),
            key_absorb,
            query_nope.reshape(8, 128),
            query_rope.reshape(8, ROPE),
            rope_cache.T,
            latent_cache,
            lengths,
            new_latent,
            new_rope,
            value_up,
        ))
    )
    latent_decode, rope_decode, attention = pl.pallas_call(
        unpack_kernel,
        grid=(2,),
        out_shape=(
            jax.ShapeDtypeStruct((TOK, LAT), BF16),
            jax.ShapeDtypeStruct((ROPE, TOK), BF16),
            jax.ShapeDtypeStruct((8, 128), BF16),
        ),
        in_specs=[
            pl.BlockSpec((CTX * MSG // 2, LAT), lambda i: (i, 0)),
            pl.BlockSpec((8, 128), lambda i: (0, 0)),
        ],
        out_specs=(
            pl.BlockSpec((TOK // 2, LAT), lambda i: (i, 0)),
            pl.BlockSpec((ROPE, TOK // 2), lambda i: (0, i)),
            pl.BlockSpec((8, 128), lambda i: (0, 0)),
        ),
        name="unpack",
        compiler_params=pltpu.CompilerParams(vmem_limit_bytes=24 << 20),
    )(land, attention)
    return attention.reshape(query_nope.shape), latent_decode, rope_decode.T


def solution(mesh):
    placed = (
        P(("req", "ctx"), None),
        P(("req", "ctx"), None),
        P("req"),
        P(("req", "ctx")),
        P(None, "req", "ctx", None),
        P(None, "req", "ctx", None),
        P(None, "req", None),
        P(None, "req", None),
        P("ctx", None, None),
        P("ctx", None, None),
    )
    return jax.shard_map(
        local,
        mesh=mesh,
        in_specs=placed,
        out_specs=(P(None, "req", "ctx", None), P(("req", "ctx"), None), P(("req", "ctx"), None)),
        check_vma=False,
    )
```

```python
import functools
import math

import jax
import jax.numpy as jnp
from jax import lax
from jax.experimental import pallas as pl
from jax.experimental.pallas import tpu as pltpu
from jax.sharding import PartitionSpec as P

NEG = -1e30
NX = 4
NZ = 8
CTX = NX * NZ
PER = 56
MSG = 64
LAT = 512
ROPE = 64
TOK = PER * CTX
HALF = 384
F32 = jnp.float32
BF16 = jnp.bfloat16
MESH = pl.DeviceIdType.MESH


def iota(shape, dim):
    return lax.broadcasted_iota(jnp.int32, shape, dim)


def pieces(column):
    first = column.astype(BF16).astype(F32)
    rest = column - first
    second = rest.astype(BF16).astype(F32)
    return first, second, rest - second


def pack_part(num, peak, den):
    rows = num.shape[0]
    lane = iota((rows, 128), 1)
    stats = jnp.zeros((rows, 128), F32)
    for at, column in enumerate(pieces(peak) + pieces(den)):
        stats = jnp.where(lane == at, column, stats)
    low = jnp.concatenate([num[:, HALF:], stats, jnp.zeros((rows, 128), F32)], axis=1)
    top = num[:, :HALF].reshape(rows // 8, 8, HALF)
    low = low.reshape(rows // 8, 8, HALF)
    return jnp.concatenate([top, low], axis=1).astype(BF16)


def halves(message):
    n = message.shape[0]
    value = message.astype(F32)
    top = value[:, :8, :].reshape(n * 8, HALF)
    low = value[:, 8:, :].reshape(n * 8, HALF)
    return top, low


def unpack_part(message):
    top, low = halves(message)
    num = jnp.concatenate([top, low[:, :128]], axis=1)
    peak = low[:, 128:129] + low[:, 129:130] + low[:, 130:131]
    den = low[:, 131:132] + low[:, 132:133] + low[:, 133:134]
    return num, peak, den


def join_parts(parts):
    peak = functools.reduce(jnp.maximum, [p[1] for p in parts])
    num = den = 0.0
    for one in parts:
        factor = jnp.exp(one[1] - peak)
        num = num + one[0] * factor
        den = den + one[2] * factor
    return num, peak, den


def exchange_kernel(
    scale,
    tgt_hbm, ka_hbm, qn_hbm, qr_hbm, rope_hbm, lat_hbm, len_hbm, nl_hbm, nr_hbm, vu_hbm,
    land_ref, att_ref,
    tgt_ref, ka_ref, qn_ref, qr_ref, rope, lat, len_ref, nl_ref, nr_ref, vu_ref, rope_t, pos, outbox, qz, qx, ql_s, qr_s, sc, wb, ca_src, ca_dst, cb_src, cb_dst,
    in_sem, own_sem, send_sem, recv_sem, qa_s, qa_r, qb_s, qb_r, ca_s, ca_r, cb_s, cb_r,
):
    me = lax.axis_index("ctx")
    z = me // NX
    x = lax.rem(me, NX)

    def along_z(k):
        return lax.rem(z + k + NZ, NZ)

    def along_x(k):
        return lax.rem(x + k, NX)

    loads = [
        pltpu.make_async_copy(src, dst, in_sem.at[i])
        for i, (src, dst) in enumerate(
            (
                (tgt_hbm, tgt_ref),
                (ka_hbm, ka_ref),
                (qn_hbm, qn_ref),
                (qr_hbm, qr_ref),
                (rope_hbm, rope),
                (lat_hbm, lat),
                (len_hbm, len_ref),
                (nl_hbm, nl_ref),
                (nr_hbm, nr_ref),
                (vu_hbm, vu_ref),
            )
        )
    ]
    for load in loads:
        load.start()

    barrier = pltpu.get_barrier_semaphore()

    def greet(i, carry):
        pl.semaphore_signal(
            barrier, inc=1, device_id={"ctx": lax.rem(me + i, CTX)}, device_id_type=MESH
        )
        return carry

    lax.fori_loop(1, CTX, greet, 0)

    for load in loads[1:4]:
        load.wait()
    qn = qn_ref[...]
    row8 = iota((8, LAT), 0)
    ql = jnp.where(
        lax.rem(row8, 2) == 0,
        jnp.dot(qn, ka_ref[0], preferred_element_type=F32),
        jnp.dot(qn, ka_ref[1], preferred_element_type=F32),
    )
    ql = ql.astype(BF16).astype(F32)
    qr = jnp.concatenate([qr_ref[...].astype(F32), jnp.zeros((8, 256 - ROPE), F32)], axis=1)
    own_query = jnp.concatenate(
        [ql[:, :HALF], jnp.concatenate([ql[:, HALF:], qr], axis=1)], axis=0
    ).astype(BF16)
    qz[z] = own_query

    loads[0].wait()
    shard = iota((CTX, 128), 0)
    hot = [(tgt_ref[b : b + 1, :] == shard).astype(F32) for b in range(TOK // 128)]
    before = (iota((128, 128), 0) < iota((128, 128), 1)).astype(BF16)
    prefix = jnp.dot(
        jnp.concatenate(hot, axis=0).astype(BF16), before, preferred_element_type=F32
    )
    base = (MSG * shard).astype(F32)
    for b in range(TOK // 128):
        part = hot[b]
        place = jnp.sum(part * (prefix[CTX * b : CTX * (b + 1)] + base), axis=0, keepdims=True)
        pos[0:1, 128 * b : 128 * (b + 1)] = place.astype(jnp.int32)
        base = base + jnp.sum(part, axis=1, keepdims=True)

    loads[4].wait()
    rope_t[...] = jnp.transpose(rope[...].astype(F32)).astype(BF16)
    loads[5].wait()

    def shard_of(i, k):
        step = (i + 1) // 2 * (2 * lax.rem(i, 2) - 1) + 2 * k
        return lax.rem(z + step + NZ, NZ) * NX + along_x(k)

    rows = NX * MSG

    def build(i):
        row = iota((rows, 1), 0)
        place = lax.rem(row, MSG)
        for k in range(NX):
            place = place + jnp.where(row // MSG == k, MSG * shard_of(i, k), 0)
        one_hot = (pos[0:1, :] == place).astype(F32).astype(BF16)
        moved = jnp.dot(one_hot, lat[...], preferred_element_type=F32)
        turned = jnp.dot(one_hot, rope_t[...], preferred_element_type=F32)
        for j in range(NX):
            block = turned[MSG * j : MSG * (j + 1)]
            packed = jnp.concatenate([block[8 * k : 8 * (k + 1)] for k in range(8)], axis=1)
            whole = jnp.concatenate([moved[MSG * j : MSG * j + PER], packed], axis=0)
            outbox[pl.ds(pl.multiple_of(MSG * shard_of(i, j), MSG), MSG), :] = whole.astype(BF16)

    def message(i, k):
        there = shard_of(i, k)
        return pltpu.make_async_remote_copy(
            src_ref=outbox.at[pl.ds(pl.multiple_of(there * MSG, MSG), MSG)],
            dst_ref=land_ref.at[pl.ds(pl.multiple_of(me * MSG, MSG), MSG)],
            send_sem=send_sem.at[there],
            recv_sem=recv_sem.at[me],
            device_id={"ctx": there},
            device_id_type=MESH,
        )

    def send(i, low=0):
        for k in range(low, NX):
            message(i, k).start()

    def build_send(i, carry):
        build(i)
        send(i)
        return carry

    build(jnp.int32(0))
    pl.semaphore_wait(barrier, CTX - 1)

    def spread_z(src, dst, s_sem, r_sem, k, own):
        there = along_z(k)
        return pltpu.make_async_remote_copy(
            src_ref=src.at[z if own else there],
            dst_ref=dst.at[z],
            send_sem=s_sem.at[k],
            recv_sem=r_sem.at[k],
            device_id={"ctx": there * NX + x},
            device_id_type=MESH,
        )

    def spread_x(src, dst, s_sem, r_sem, k, own):
        there = along_x(k)
        return pltpu.make_async_remote_copy(
            src_ref=src if own else src.at[there],
            dst_ref=dst.at[x],
            send_sem=s_sem.at[k],
            recv_sem=r_sem.at[k],
            device_id={"ctx": z * NX + there},
            device_id_type=MESH,
        )

    def arrive_z(dst, r_sem, s_sem, k):
        return pltpu.make_async_remote_copy(
            src_ref=dst.at[z],
            dst_ref=dst.at[along_z(NZ - k)],
            send_sem=s_sem.at[k],
            recv_sem=r_sem.at[k],
            device_id={"ctx": along_z(k) * NX + x},
            device_id_type=MESH,
        )

    def arrive_x(dst, r_sem, s_sem, k):
        return pltpu.make_async_remote_copy(
            src_ref=dst.at[x],
            dst_ref=dst.at[along_x(NX - k)],
            send_sem=s_sem.at[k],
            recv_sem=r_sem.at[k],
            device_id={"ctx": z * NX + along_x(k)},
            device_id_type=MESH,
        )

    for k in range(1, NZ):
        spread_z(qz, qz, qa_s, qa_r, k, True).start()
    send(jnp.int32(0), 1)
    lax.fori_loop(1, 3, build_send, 0)

    for k in range(1, NZ):
        arrive_z(qz, qa_r, qa_s, k).wait_recv()
    for k in range(1, NX):
        spread_x(qz, qx, qb_s, qb_r, k, True).start()
    qx[x] = qz[...]
    lax.fori_loop(3, 8, build_send, 0)
    for k in range(1, NX):
        arrive_x(qx, qb_r, qb_s, k).wait_recv()

    for s in range(NX):
        top, low = halves(qx[s])
        ql_s[64 * s : 64 * (s + 1), :] = jnp.concatenate([top, low[:, :128]], axis=1).astype(BF16)
        qr_s[64 * s : 64 * (s + 1), :] = low[:, 128 : 128 + ROPE].astype(BF16)
    heads = 8 * CTX
    chunk = 256
    loads[6].wait()
    bound = len_ref[0] - me * TOK
    row_request = lax.rem(iota((heads, chunk), 0) // 2, 2)
    peak = jnp.full((heads, 1), NEG, F32)
    for c in range(TOK // chunk):
        at = slice(chunk * c, chunk * (c + 1))
        scores = lax.dot_general(
            ql_s[...], lat[at, :], (((1,), (1,)), ((), ())), preferred_element_type=F32
        ) + jnp.dot(qr_s[...], rope[:, at], preferred_element_type=F32)
        token_request = (iota((heads, chunk), 1) + chunk * c >= bound).astype(jnp.int32)
        scores = jnp.where(token_request == row_request, scores * scale, NEG)
        sc[:, at] = scores
        peak = jnp.maximum(peak, jnp.max(scores, axis=1, keepdims=True))
    den = jnp.zeros((heads, 1), F32)
    for c in range(TOK // chunk):
        at = slice(chunk * c, chunk * (c + 1))
        scores = sc[:, at]
        weight = jnp.where(scores > 0.5 * NEG, jnp.exp(scores - peak), 0.0)
        den = den + jnp.sum(weight, axis=1, keepdims=True)
        wb[:, at] = weight.astype(BF16)
    num = jnp.dot(wb[...], lat[...], preferred_element_type=F32)
    for s in range(NX):
        at = slice(64 * s, 64 * (s + 1))
        ca_src[s] = pack_part(num[at], peak[at], den[at])

    for k in range(1, NX):
        spread_x(ca_src, ca_dst, ca_s, ca_r, k, False).start()
    ca_dst[x] = ca_src[x]

    for k in range(1, NX):
        arrive_x(ca_dst, ca_r, ca_s, k).wait_recv()
    cb_src[...] = pack_part(*join_parts([unpack_part(ca_dst[s]) for s in range(NX)]))
    for k in range(1, NZ):
        spread_z(cb_src, cb_dst, cb_s, cb_r, k, False).start()
    cb_dst[z] = cb_src[z]
    mine = pl.ds(pl.multiple_of(me * MSG, MSG), MSG)
    keep = pltpu.make_async_copy(outbox.at[mine], land_ref.at[mine], own_sem)
    keep.start()

    top, low = halves(qz[pl.ds(z, 1)])
    own_ql = jnp.concatenate([top, low[:, :128]], axis=1)
    own_qr = low[:, 128 : 128 + ROPE]
    row_at = iota((8, 1), 0)
    fresh = []
    for load in loads[7:]:
        load.wait()
    for f in range(4):
        key_latent = nl_ref[f // 2].astype(F32)[f % 2 : f % 2 + 1, :]
        key_rope = nr_ref[f // 2].astype(F32)[f % 2 : f % 2 + 1, :]
        score = (
            jnp.sum(own_ql * key_latent, axis=1, keepdims=True)
            + jnp.sum(own_qr * key_rope, axis=1, keepdims=True)
        ) * scale
        usable = (f // 2 <= row_at // 4) & (f % 2 == lax.rem(row_at // 2, 2))
        fresh.append((usable, jnp.where(usable, score, NEG), key_latent))

    for k in range(1, NZ):
        arrive_z(cb_dst, cb_r, cb_s, k).wait_recv()
    num, peak, den = join_parts([unpack_part(cb_dst[pl.ds(s, 1)]) for s in range(NZ)])
    top_peak = functools.reduce(jnp.maximum, [one[1] for one in fresh], peak)
    factor = jnp.exp(peak - top_peak)
    num = num * factor
    den = den * factor
    for usable, score, key_latent in fresh:
        weight = jnp.where(usable, jnp.exp(score - top_peak), 0.0)
        den = den + weight
        num = num + weight.astype(BF16).astype(F32) * key_latent
    latent_out = (num / den).astype(BF16)
    att_ref[...] = jnp.where(
        lax.rem(iota((8, 128), 0), 2) == 0,
        jnp.dot(latent_out, vu_ref[0], preferred_element_type=F32),
        jnp.dot(latent_out, vu_ref[1], preferred_element_type=F32),
    ).astype(BF16)

    def settle(i, carry):
        there = lax.rem(me + i, CTX)
        one = pltpu.make_async_remote_copy(
            src_ref=outbox.at[pl.ds(pl.multiple_of(there * MSG, MSG), MSG)],
            dst_ref=land_ref.at[pl.ds(pl.multiple_of(there * MSG, MSG), MSG)],
            send_sem=send_sem.at[there],
            recv_sem=recv_sem.at[there],
            device_id={"ctx": there},
            device_id_type=MESH,
        )
        one.wait_send()
        one.wait_recv()
        return carry

    lax.fori_loop(1, CTX, settle, 0)
    keep.wait()
    for k in range(1, NZ):
        spread_z(qz, qz, qa_s, qa_r, k, True).wait_send()
        spread_z(cb_src, cb_dst, cb_s, cb_r, k, False).wait_send()
    for k in range(1, NX):
        spread_x(qz, qx, qb_s, qb_r, k, True).wait_send()
        spread_x(ca_src, ca_dst, ca_s, ca_r, k, False).wait_send()


def unpack_kernel(land_ref, part_ref, lat_ref, rope_ref, att_ref):
    att_ref[...] = part_ref[...]
    turned = []
    for s in range(0, land_ref.shape[0] // MSG, 2):
        both = []
        for at in (MSG * s, MSG * (s + 1)):
            value = land_ref[at : at + MSG, :].astype(F32)
            both.append(value[:PER])
            packed = value[PER:]
            turned += [packed[:, ROPE * k : ROPE * (k + 1)] for k in range(PER // 8)]
        lat_ref[PER * s : PER * (s + 2), :] = jnp.concatenate(both, axis=0).astype(BF16)
    rope_ref[...] = jnp.transpose(jnp.concatenate(turned, axis=0)).astype(BF16)


def local(
    latent_cache,
    rope_cache,
    lengths,
    target_shard,
    query_nope,
    query_rope,
    new_latent,
    new_rope,
    key_absorb,
    value_up,
):
    scale = 1.0 / math.sqrt(query_nope.shape[3] + ROPE)
    vmem = pl.BlockSpec(memory_space=pltpu.VMEM)
    hbm = pl.BlockSpec(memory_space=pltpu.HBM)
    anywhere = pl.BlockSpec(memory_space=pl.ANY)
    dma = pltpu.SemaphoreType.DMA
    land, attention = pl.pallas_call(
        functools.partial(exchange_kernel, scale),
        out_shape=(
            pltpu.VMEM((CTX * MSG, LAT), BF16),
            pltpu.VMEM((8, 128), BF16),
        ),
        in_specs=[hbm] * 10,
        out_specs=(anywhere, vmem),
        scratch_shapes=[
            pltpu.VMEM((TOK // 128, 128), jnp.int32),
            pltpu.VMEM(key_absorb.shape, BF16),
            pltpu.VMEM((8, 128), BF16),
            pltpu.VMEM((8, ROPE), BF16),
            pltpu.VMEM((ROPE, TOK), BF16),
            pltpu.VMEM((TOK, LAT), BF16),
            pltpu.SMEM((2,), jnp.int32),
            pltpu.VMEM(new_latent.shape, BF16),
            pltpu.VMEM(new_rope.shape, BF16),
            pltpu.VMEM(value_up.shape, BF16),
            pltpu.VMEM((TOK, ROPE), BF16),
            pltpu.VMEM((8, TOK), jnp.int32),
            pltpu.VMEM((CTX * MSG, LAT), BF16),
            pltpu.VMEM((NZ, 16, HALF), BF16),
            pltpu.VMEM((NX, NZ, 16, HALF), BF16),
            pltpu.VMEM((8 * CTX, LAT), BF16),
            pltpu.VMEM((8 * CTX, ROPE), BF16),
            pltpu.VMEM((8 * CTX, TOK), F32),
            pltpu.VMEM((8 * CTX, TOK), BF16),
            pltpu.VMEM((NX, NZ, 16, HALF), BF16),
            pltpu.VMEM((NX, NZ, 16, HALF), BF16),
            pltpu.VMEM((NZ, 16, HALF), BF16),
            pltpu.VMEM((NZ, 16, HALF), BF16),
            dma((10,)),
            dma,
            dma((CTX,)),
            dma((CTX,)),
            dma((NZ,)),
            dma((NZ,)),
            dma((NX,)),
            dma((NX,)),
            dma((NX,)),
            dma((NX,)),
            dma((NZ,)),
            dma((NZ,)),
        ],
        name="exchange",
        compiler_params=pltpu.CompilerParams(
            collective_id=1, has_side_effects=True, vmem_limit_bytes=40 << 20
        ),
    )(
        *(pltpu.with_memory_space_constraint(array, pltpu.HBM) for array in (
            target_shard.reshape(TOK // 128, 128),
            key_absorb,
            query_nope.reshape(8, 128),
            query_rope.reshape(8, ROPE),
            rope_cache.T,
            latent_cache,
            lengths,
            new_latent,
            new_rope,
            value_up,
        ))
    )
    latent_decode, rope_decode, attention = pl.pallas_call(
        unpack_kernel,
        grid=(2,),
        out_shape=(
            jax.ShapeDtypeStruct((TOK, LAT), BF16),
            jax.ShapeDtypeStruct((ROPE, TOK), BF16),
            jax.ShapeDtypeStruct((8, 128), BF16),
        ),
        in_specs=[
            pl.BlockSpec((CTX * MSG // 2, LAT), lambda i: (i, 0)),
            pl.BlockSpec((8, 128), lambda i: (0, 0)),
        ],
        out_specs=(
            pl.BlockSpec((TOK // 2, LAT), lambda i: (i, 0)),
            pl.BlockSpec((ROPE, TOK // 2), lambda i: (0, i)),
            pl.BlockSpec((8, 128), lambda i: (0, 0)),
        ),
        name="unpack",
        compiler_params=pltpu.CompilerParams(vmem_limit_bytes=24 << 20),
    )(land, attention)
    return attention.reshape(query_nope.shape), latent_decode, rope_decode.T


def solution(mesh):
    placed = (
        P(("req", "ctx"), None),
        P(("req", "ctx"), None),
        P("req"),
        P(("req", "ctx")),
        P(None, "req", "ctx", None),
        P(None, "req", "ctx", None),
        P(None, "req", None),
        P(None, "req", None),
        P("ctx", None, None),
        P("ctx", None, None),
    )
    return jax.shard_map(
        local,
        mesh=mesh,
        in_specs=placed,
        out_specs=(P(None, "req", "ctx", None), P(("req", "ctx"), None), P(("req", "ctx"), None)),
        check_vma=False,
    )
```
